128 devices in a mesh: inp: 4 (over y_hi, core), wt: 4 (over x), out: 8 (over y_lo, z).
Axes of the slice: x: 4, y: 4 (y_hi: 2, y_lo: 2; y = y_hi * 2 + y_lo), z: 4, core: 2. Of those that a mesh axis runs over, the one named last changes fastest.
Arguments:
- tokens: bfloat16 [2, 4096, 2048], P(None, ('inp', 'wt'), 'out'), may hold values from -6 to 6
- gate_weight: bfloat16 [2048, 4096], P('out', ('wt', 'inp')), may hold values from -0.125 to 0.125
- up_weight: bfloat16 [2048, 4096], P('out', ('wt', 'inp')), may hold values from -0.125 to 0.125
- down_weight: bfloat16 [4096, 2048], P(('wt', 'inp'), 'out'), may hold values from -0.09375 to 0.09375
- cotangent: bfloat16 [2, 4096, 2048], P(None, ('inp', 'wt'), 'out'), may hold values from -3 to 3
Outputs:
- output: bfloat16 [2, 4096, 2048], P(None, ('inp', 'wt'), 'out')
- grad_tokens: bfloat16 [2, 4096, 2048], P(None, ('inp', 'wt'), 'out')
- grad_gate: float32 [2048, 4096], P('out', ('wt', 'inp'))
- grad_up: float32 [2048, 4096], P('out', ('wt', 'inp'))
- grad_down: float32 [4096, 2048], P(('wt', 'inp'), 'out')
The draws below stay inside these ranges and needn't reach their ends.
All inputs are finite; a program needn't handle non-finite values.
Results may differ from the reference program's by a relative error of at most 0.035.
Values may be sent and summed in bfloat16 or wider, within the bound.
A program may use at most 128 MiB of HBM per device.

```python
import jax
import jax.numpy as jnp
from jax import lax

D = 2048
FF = 4096
MB = 2
TOK_DEV = 1024
TOKENS = 4096
N_INP = 4
N_OUT = 8


def steps_of(stream_key, extent, split, smallest, largest):
    def one(axis_at, shards_of):
        steps = jax.random.uniform(jax.random.fold_in(jax.random.fold_in(stream_key, 6), axis_at), (shards_of,), jnp.float32, smallest / len(split), largest / len(split))
        return jnp.repeat(jnp.exp(steps), extent[axis_at] // shards_of).reshape((-1,) + (1,) * (len(extent) - axis_at - 1))

    gain = one(*split[0])
    for cut in split[1:]:
        gain = gain * one(*cut)
    return gain


def noise(own_key, extent, deviation, limit, shards=(), kind=jnp.bfloat16):
    values = deviation * jax.random.normal(own_key, extent, jnp.float32)
    if shards:
        values = values * steps_of(own_key, extent, shards, -0.22, 0.18)
    return jnp.clip(values, -limit, limit).astype(kind)


def setup_inputs(seed: int = 0) -> dict:
    key_list = jax.random.split(jax.random.key(seed), 6)
    tokens = noise(key_list[0], (MB, TOKENS, D), 1.0, 6.0, ((1, 16), (2, 8)))
    gate_weight = noise(key_list[1], (D, FF), D ** -0.5, 0.125, ((0, 8), (1, 16)))
    up_weight = noise(key_list[2], (D, FF), D ** -0.5, 0.125, ((0, 8), (1, 16)))
    down_weight = noise(key_list[3], (FF, D), FF ** -0.5, 0.09375, ((0, 16), (1, 8)))
    cotangent = noise(key_list[4], (MB, TOKENS, D), 0.5, 3.0, ((1, 16), (2, 8)))
    return {"tokens": tokens, "gate_weight": gate_weight, "up_weight": up_weight, "down_weight": down_weight, "cotangent": cotangent}


def rounded(value):
    return lax.optimization_barrier(value.astype(jnp.bfloat16)).astype(jnp.float32)


def group_rows(array, group):
    batches = array.shape[0]
    shaped = array.reshape(batches, N_INP, TOK_DEV, array.shape[2])
    return shaped[:, group].reshape(batches * TOK_DEV, array.shape[2])


def reference(tokens, gate_weight, up_weight, down_weight, cotangent):
    batches, length, model_dim = tokens.shape
    hidden_dim = gate_weight.shape[1]
    flat_in = tokens.reshape(batches * length, model_dim)
    flat_cot = cotangent.reshape(batches * length, model_dim)
    block_cols = model_dim // N_OUT
    gate_sum = jnp.zeros((batches * length, hidden_dim), jnp.float32)
    up_sum = jnp.zeros((batches * length, hidden_dim), jnp.float32)
    back_sum = jnp.zeros((batches * length, hidden_dim), jnp.float32)
    for block in range(N_OUT):
        lower = block * block_cols
        upper = lower + block_cols
        in_cols = flat_in[:, lower:upper]
        cot_cols = flat_cot[:, lower:upper]
        gate_sum = gate_sum + rounded(jnp.dot(in_cols, gate_weight[lower:upper], preferred_element_type=jnp.float32))
        up_sum = up_sum + rounded(jnp.dot(in_cols, up_weight[lower:upper], preferred_element_type=jnp.float32))
        back_sum = back_sum + rounded(jnp.dot(cot_cols, down_weight[:, lower:upper].T, preferred_element_type=jnp.float32))
    sigmoid_g = jax.nn.sigmoid(gate_sum)
    silu_g = gate_sum * sigmoid_g
    hidden = (silu_g * up_sum).astype(jnp.bfloat16)
    slope = sigmoid_g * (1.0 + gate_sum * (1.0 - sigmoid_g))
    grad_gate_act = (back_sum * up_sum * slope).astype(jnp.bfloat16)
    grad_up_act = (back_sum * silu_g).astype(jnp.bfloat16)
    output = jnp.dot(hidden, down_weight, preferred_element_type=jnp.float32).astype(jnp.bfloat16)
    grad_flat = jnp.dot(grad_gate_act, gate_weight.T, preferred_element_type=jnp.float32)
    grad_flat = grad_flat + jnp.dot(grad_up_act, up_weight.T, preferred_element_type=jnp.float32)
    grad_tokens = grad_flat.astype(jnp.bfloat16)
    shaped_in = flat_in.reshape(batches, length, model_dim)
    shaped_cot = flat_cot.reshape(batches, length, model_dim)
    shaped_hidden = hidden.reshape(batches, length, hidden_dim)
    shaped_gate = grad_gate_act.reshape(batches, length, hidden_dim)
    shaped_up = grad_up_act.reshape(batches, length, hidden_dim)
    grad_gate = jnp.zeros((model_dim, hidden_dim), jnp.float32)
    grad_up = jnp.zeros((model_dim, hidden_dim), jnp.float32)
    grad_down = jnp.zeros((hidden_dim, model_dim), jnp.float32)
    for group in range(N_INP):
        in_group = group_rows(shaped_in, group)
        grad_gate = grad_gate + rounded(jnp.dot(in_group.T, group_rows(shaped_gate, group), preferred_element_type=jnp.float32))
        grad_up = grad_up + rounded(jnp.dot(in_group.T, group_rows(shaped_up, group), preferred_element_type=jnp.float32))
        grad_down = grad_down + rounded(jnp.dot(group_rows(shaped_hidden, group).T, group_rows(shaped_cot, group), preferred_element_type=jnp.float32))
    return (output.reshape(batches, length, model_dim), grad_tokens.reshape(batches, length, model_dim), grad_gate, grad_up, grad_down)
```

```python
import functools

import jax
import jax.numpy as jnp
from jax import lax
from jax.experimental import pallas as pl
from jax.experimental.pallas import tpu as pltpu
from jax.sharding import PartitionSpec as P

MESH = pl.DeviceIdType.MESH
BF16 = jnp.bfloat16
F32 = jnp.float32

NN = (((1,), (0,)), ((), ()))
NT = (((1,), (1,)), ((), ()))
TN = (((0,), (0,)), ((), ()))


def dot(a, b, dims):
    return lax.dot_general(a, b, dims, preferred_element_type=F32)


class Sems:
    def __init__(self, ref, size):
        self.ref, self.size, self.used = ref, size, 0

    def take(self):
        assert self.used < self.size
        self.used += 1
        return self.ref.at[self.used - 1]


N_SEND = 128
N_RECV = 96


def kernel(
    tok, gate_w, up_w, down_w, cot,
    out_ref, gtok_ref, ggate_ref, gup_ref, gdown_ref,
    down_t, xin, wts, part_own, part_out, part_in, act, res, wgr,
    rxa0, rxa1, rxb0, rxb1, ry0, ry1, sy, fin, rza, rzb, sw, hw,
    send_sems, recv_sems, hw_in,
):
    i, x, o = lax.axis_index("inp"), lax.axis_index("wt"), lax.axis_index("out")
    h, c, l, z = i // 2, i % 2, o // 4, o % 4
    p = (h + l) % 2

    def dev(h, c, x, l, z):
        return {"inp": h * 2 + c, "wt": x, "out": l * 4 + z}

    def ring(v, d):
        return (v + d + 4) % 4

    x_to = [dev(h, c, ring(x, 1), l, z), dev(h, c, ring(x, -1), l, z)]
    z_to = [dev(h, c, x, l, ring(z, 1)), dev(h, c, x, l, ring(z, -1))]
    y_to = dev(1 - h, c, x, 1 - l, z)
    core_to = dev(h, 1 - c, x, l, z)

    sends = Sems(send_sems, N_SEND)
    recvs = Sems(recv_sems, N_RECV)
    pending = []

    def send(src, dst, sem, to):
        copy = pltpu.make_async_remote_copy(
            src, dst, sends.take(), sem, device_id=to, device_id_type=MESH
        )
        copy.start()
        pending.append(copy)

    def send_or_keep(src, dst, sem, to, mine):
        copy = pltpu.make_async_remote_copy(
            src, dst, sends.take(), sem, device_id=to, device_id_type=MESH
        )

        @pl.when(mine)
        def _():
            pltpu.make_async_copy(src, dst, sem).start()

        @pl.when(jnp.logical_not(mine))
        def _():
            copy.start()

        pending.append((copy, mine))

    def arrived(ref, sem):
        pltpu.make_async_copy(ref, ref, sem).wait()

    def rows(start, size):
        return pl.ds(pl.multiple_of(start, 64), size)

    def cols(start, size):
        return pl.ds(pl.multiple_of(start, 256), size)

    barrier = pltpu.get_barrier_semaphore()
    met = 0
    for dl in range(2):
        for dz in range(4):
            for dc in range(2):
                if dl or dz or dc:
                    to = dev(h, (c + dc) % 2, x, (l + dl) % 2, ring(z, dz))
                    pl.semaphore_signal(barrier, inc=1, device_id=to, device_id_type=MESH)
                    met += 1
    for to in x_to + [y_to]:
        pl.semaphore_signal(barrier, inc=1, device_id=to, device_id_type=MESH)
        met += 1
    down_t[...] = down_w[...].T
    pl.semaphore_wait(barrier, met)

    source = [tok, cot]
    own_slot = (x * 2 + h) * 128
    x_a2a = [recvs.take(), recvs.take()]
    w_in = [recvs.take() for _ in range(3)]
    weights = [gate_w, up_w, down_t]

    def scatter(a):
        for dl, dz in ((1, 2), (0, 2), (1, 1), (1, 3), (0, 1), (0, 3), (1, 0), (0, 0)):
            lt, zt = (l + dl) % 2, ring(z, dz)
            label = ((h + lt) % 2) * 4 + zt
            src = source[a].at[rows(label * 64, 64), :]
            dst = xin.at[a, rows(own_slot + c * 64, 64), cols(z * 256, 256)]
            to = dev(h, l, x, lt, zt)
            if dl or dz:
                send(src, dst, x_a2a[a], to)
            else:
                send_or_keep(src, dst, x_a2a[a], to, c == l)

    def spread_weight(w):
        dst = wts.at[w, rows(z * 256, 256), cols(c * 256, 256)]
        send(weights[w], dst, w_in[w], dev(h, l, x, 1 - l, z))
        send_or_keep(weights[w], dst, w_in[w], dev(h, l, x, l, z), c == l)

    scatter(1)
    spread_weight(0)
    scatter(0)
    spread_weight(1)
    spread_weight(2)

    def x_slot(a, dx, other=False, start=0, size=128):
        hh = 1 - h if other else h
        return xin.at[a, rows((ring(x, dx) * 2 + hh) * 128 + start, size), :]

    y_x0 = recvs.take()
    y_x1 = [recvs.take() for _ in range(4)]
    x_hop = {
        key: [[recvs.take(), recvs.take()], [recvs.take(), recvs.take()]]
        for key in ((1, False), (0, False), (0, True))
    }
    z_hop = [[[recvs.take(), recvs.take()], [recvs.take(), recvs.take()]] for _ in range(3)]

    def x_first(a, other):
        for d in range(2):
            ref = x_slot(a, 0, other)
            send(ref, ref, x_hop[a, other][0][d], x_to[d])

    def x_second(a, other):
        for d, dx in ((0, -1), (1, 1)):
            arrived(x_slot(a, dx, other), x_hop[a, other][0][d])
            ref = x_slot(a, dx, other, 64 * d, 64)
            send(ref, ref, x_hop[a, other][1][d], x_to[d])

    def x_last(a, other):
        for d in range(2):
            arrived(x_slot(a, 2, other, 64 * d, 64), x_hop[a, other][1][d])

    def w_block(w, dz, start=0, size=256):
        return wts.at[w, rows(ring(z, dz) * 256 + start, size), :]

    def z_first(w):
        arrived(w_block(w, 0), w_in[w])
        for d in range(2):
            send(w_block(w, 0), w_block(w, 0), z_hop[w][0][d], z_to[d])

    def z_second(w):
        for d, dz in ((0, -1), (1, 1)):
            arrived(w_block(w, dz), z_hop[w][0][d])
            ref = w_block(w, dz, 128 * d, 128)
            send(ref, ref, z_hop[w][1][d], z_to[d])

    def z_last(w):
        for d in range(2):
            arrived(w_block(w, 2, 128 * d, 128), z_hop[w][1][d])

    def y_send(dx):
        send(x_slot(1, dx), x_slot(1, dx), y_x1[dx % 4], y_to)

    z_first(0)
    arrived(x_slot(1, 0), x_a2a[1])
    x_first(1, False)
    arrived(x_slot(0, 0), x_a2a[0])
    send(x_slot(0, 0), x_slot(0, 0), y_x0, y_to)
    x_first(0, False)
    y_send(0)
    z_first(1)
    z_first(2)
    x_second(1, False)
    y_send(-1)
    y_send(1)
    arrived(x_slot(0, 0, True), y_x0)
    x_first(0, True)
    z_second(0)
    x_second(0, False)
    z_second(1)
    x_last(1, False)
    y_send(2)
    x_second(0, True)
    z_second(2)
    x_last(0, False)
    for w in range(3):
        z_last(w)

    p_in = [recvs.take() for _ in range(4)]
    a_in = [recvs.take() for _ in range(4)]

    def products(dx):
        arrived(x_slot(1, dx, True), y_x1[dx % 4])
        base = ring(x, dx) * 256
        mine, theirs = base + c * 128, base + (1 - c) * 128
        for w in range(3):
            lhs = jnp.concatenate(
                [xin[w // 2, rows(mine, 128), :], xin[w // 2, rows(theirs, 128), :]], axis=0
            )
            r = dot(lhs, wts[w], NN)
            part_own[dx % 4, w] = r[:128]
            part_out[dx % 4, w] = r[128:].astype(BF16)
        send(part_out.at[dx % 4], part_in.at[dx % 4], p_in[dx % 4], core_to)

    def activate(dx):
        g = dx % 4
        arrived(part_in.at[g], p_in[g])
        mine = ring(x, dx) * 256 + c * 128
        gate = part_own[g, 0] + part_in[g, 0].astype(F32)
        up = part_own[g, 1] + part_in[g, 1].astype(F32)
        back = part_own[g, 2] + part_in[g, 2].astype(F32)
        s = jax.nn.sigmoid(gate)
        silu = gate * s
        act[0, rows(mine, 128), :] = (back * up * (s * (1.0 + gate * (1.0 - s)))).astype(BF16)
        act[1, rows(mine, 128), :] = (back * silu).astype(BF16)
        act[2, rows(mine, 128), :] = (silu * up).astype(BF16)
        ref = act.at[:, rows(mine, 128), :]
        send(ref, ref, a_in[g], core_to)

    def act_ready(dx):
        theirs = ring(x, dx) * 256 + (1 - c) * 128
        arrived(act.at[:, rows(theirs, 128), :], a_in[dx % 4])

    products(0)
    products(1)
    activate(0)
    products(-1)
    activate(1)
    x_last(0, True)
    products(2)
    activate(-1)
    activate(2)

    def backward(dx):
        at = rows(ring(x, dx) * 256, 256)
        r = dot(act[0, at, :], wts[0], NT) + dot(act[1, at, :], wts[1], NT)
        res[1, at, :] = r.astype(BF16)
        send(r_slot(1, dx, True), ry1.at[dx % 4], ry1_in[dx % 4], y_to)
        r = dot(act[2, at, :], wts[2], NT)
        res[0, at, :] = r.astype(BF16)

    def r_group(dx, start=0, size=256):
        return res.at[0, rows(ring(x, dx) * 256 + start, size), :]

    def r_slot(a, dx, other=False, start=0, size=128):
        hh = 1 - h if other else h
        return res.at[a, rows((ring(x, dx) * 2 + hh) * 128 + start, size), :]

    def add_into(ref, inc):
        ref[...] = (ref[...].astype(F32) + inc[...].astype(F32)).astype(BF16)

    def take2():
        return [recvs.take(), recvs.take()]

    ry0_in = recvs.take()
    ry1_in = [recvs.take() for _ in range(4)]
    rxa0_in, rxa1_in, rxb0_in, rxb1_in = take2(), take2(), take2(), take2()
    rza_in = [take2() for _ in range(3)]
    rzb_in = [take2() for _ in range(3)]
    home_in = take2()

    def summed1(dx):
        arrived(ry1.at[dx % 4], ry1_in[dx % 4])
        add_into(r_slot(1, dx), ry1.at[dx % 4])

    def g_block(w, dz, start=0, size=256):
        return wgr.at[w, rows(ring(z, dz) * 256 + start, size), :]

    def weight_grads(dz):
        at = cols(ring(z, dz) * 256, 256)
        for w in range(3):
            r = dot(xin[w // 2, :, at], act[w], TN)
            g_block(w, dz)[...] = r.astype(BF16)

    def z_step1():
        for w in range(3):
            for d in range(2):
                send(g_block(w, 2, 128 * d, 128), rza.at[w, d], rza_in[w][d], z_to[d])

    def z_step2(d, dz):
        for w in range(3):
            arrived(rza.at[w, d], rza_in[w][d])
            add_into(g_block(w, dz, 128 * d, 128), rza.at[w, d])
            send(g_block(w, dz), rzb.at[w, d], rzb_in[w][d], z_to[d])

    act_ready(2)
    backward(2)
    for d in range(2):
        send(r_group(2, 128 * d, 128), rxa0.at[d], rxa0_in[d], x_to[d])
    act_ready(0)
    act_ready(1)
    act_ready(-1)
    weight_grads(2)
    z_step1()
    summed1(2)
    for d in range(2):
        send(r_slot(1, 2, False, 64 * d, 64), rxa1.at[d], rxa1_in[d], x_to[d])
    for d, dx in ((0, 1), (1, -1)):
        backward(dx)
        arrived(rxa0.at[d], rxa0_in[d])
        add_into(r_group(dx, 128 * d, 128), rxa0.at[d])
        send(r_group(dx), rxb0.at[d], rxb0_in[d], x_to[d])
        weight_grads(dx)
        z_step2(d, dx)
    for d, dx in ((0, 1), (1, -1)):
        summed1(dx)
        arrived(rxa1.at[d], rxa1_in[d])
        add_into(r_slot(1, dx, False, 64 * d, 64), rxa1.at[d])
        send(r_slot(1, dx), rxb1.at[d], rxb1_in[d], x_to[d])
    backward(0)
    weight_grads(0)
    summed1(0)

    for d in range(2):
        arrived(rxb0.at[d], rxb0_in[d])
    other = r_group(0, (1 - h) * 128, 128)
    sy[...] = (
        other[...].astype(F32)
        + rxb0[0, rows((1 - h) * 128, 128), :].astype(F32)
        + rxb0[1, rows((1 - h) * 128, 128), :].astype(F32)
    ).astype(BF16)
    send(sy, ry0, ry0_in, y_to)

    home = [out_ref, gtok_ref]

    def go_home(a):
        for dz in (2, 1, 3, 0):
            for dc in (1, 0):
                zt, ct = ring(z, dz), (c + dc) % 2
                src = fin.at[a, rows(ct * 64, 64), cols(zt * 256, 256)]
                dst = home[a].at[rows((p * 4 + z) * 64, 64), :]
                to = dev(h, ct, x, c, zt)
                if dz or dc:
                    send(src, dst, home_in[a], to)
                else:
                    send_or_keep(src, dst, home_in[a], to, c == l)

    for d in range(2):
        arrived(rxb1.at[d], rxb1_in[d])
    fin[1] = (
        r_slot(1, 0)[...].astype(F32) + rxb1[0].astype(F32) + rxb1[1].astype(F32)
    ).astype(BF16)
    go_home(1)

    for w in range(3):
        for d in range(2):
            arrived(rzb.at[w, d], rzb_in[w][d])
        sw[w] = (
            g_block(w, 0)[...].astype(F32) + rzb[w, 0].astype(F32) + rzb[w, 1].astype(F32)
        ).astype(BF16)
    for dc in (1, 0):
        ct = (c + dc) % 2
        src = sw.at[:, :, cols(ct * 256, 256)]
        to = dev(h, ct, x, c, z)
        if dc:
            send(src, hw.at[l], hw_in.at[l], to)
        else:
            send_or_keep(src, hw.at[l], hw_in.at[l], to, c == l)

    arrived(ry0, ry0_in)
    at = rows(h * 128, 128)
    fin[0] = (
        r_slot(0, 0)[...].astype(F32)
        + rxb0[0, at, :].astype(F32)
        + rxb0[1, at, :].astype(F32)
        + ry0[...].astype(F32)
    ).astype(BF16)
    go_home(0)

    for ls in range(2):
        arrived(hw.at[ls], hw_in.at[ls])
    ggate_ref[...] = hw[0, 0].astype(F32) + hw[1, 0].astype(F32)
    gup_ref[...] = hw[0, 1].astype(F32) + hw[1, 1].astype(F32)
    gdown_ref[...] = (hw[0, 2].astype(F32) + hw[1, 2].astype(F32)).T
    for a in (1, 0):
        arrived(home[a], home_in[a])

    for item in pending:
        if isinstance(item, tuple):
            copy, mine = item

            @pl.when(jnp.logical_not(mine))
            def _(copy=copy):
                copy.wait_send()
        else:
            item.wait_send()


def on_device(tokens, gate_weight, up_weight, down_weight, cotangent):
    vmem = pl.BlockSpec(memory_space=pltpu.VMEM)
    results = pl.pallas_call(
        kernel,
        name="swiglu",
        out_shape=[jax.ShapeDtypeStruct((512, 256), BF16)] * 2
        + [jax.ShapeDtypeStruct((256, 256), F32)] * 3,
        in_specs=[vmem] * 5,
        out_specs=[vmem] * 5,
        scratch_shapes=[
            pltpu.VMEM((256, 256), BF16),
            pltpu.VMEM((2, 1024, 1024), BF16),
            pltpu.VMEM((3, 1024, 512), BF16),
            pltpu.VMEM((4, 3, 128, 512), F32),
            pltpu.VMEM((4, 3, 128, 512), BF16),
            pltpu.VMEM((4, 3, 128, 512), BF16),
            pltpu.VMEM((3, 1024, 512), BF16),
            pltpu.VMEM((2, 1024, 1024), BF16),
            pltpu.VMEM((3, 1024, 512), BF16),
            pltpu.VMEM((2, 128, 1024), BF16),
            pltpu.VMEM((2, 64, 1024), BF16),
            pltpu.VMEM((2, 256, 1024), BF16),
            pltpu.VMEM((2, 128, 1024), BF16),
            pltpu.VMEM((128, 1024), BF16),
            pltpu.VMEM((4, 128, 1024), BF16),
            pltpu.VMEM((128, 1024), BF16),
            pltpu.VMEM((2, 128, 1024), BF16),
            pltpu.VMEM((3, 2, 128, 512), BF16),
            pltpu.VMEM((3, 2, 256, 512), BF16),
            pltpu.VMEM((3, 256, 512), BF16),
            pltpu.VMEM((2, 3, 256, 256), BF16),
            pltpu.SemaphoreType.DMA((N_SEND,)),
            pltpu.SemaphoreType.DMA((N_RECV,)),
            pltpu.SemaphoreType.DMA((2,)),
        ],
        compiler_params=pltpu.CompilerParams(
            collective_id=0, has_side_effects=True, vmem_limit_bytes=60 << 20
        ),
        cost_estimate=pl.CostEstimate(
            flops=9 * 2 * 1024 * 1024 * 512, bytes_accessed=3 << 20, transcendentals=1024 * 256
        ),
    )(
        tokens.reshape(512, 256),
        gate_weight,
        up_weight,
        down_weight,
        cotangent.reshape(512, 256),
    )
    output, grad_tokens, grad_gate, grad_up, grad_down = results
    return (
        output.reshape(2, 256, 256),
        grad_tokens.reshape(2, 256, 256),
        grad_gate,
        grad_up,
        grad_down,
    )


def solution(mesh):
    in_specs = (
        P(None, ("inp", "wt"), "out"),
        P("out", ("wt", "inp")),
        P("out", ("wt", "inp")),
        P(("wt", "inp"), "out"),
        P(None, ("inp", "wt"), "out"),
    )
    out_specs = (
        P(None, ("inp", "wt"), "out"),
        P(None, ("inp", "wt"), "out"),
        P("out", ("wt", "inp")),
        P("out", ("wt", "inp")),
        P(("wt", "inp"), "out"),
    )
    return jax.shard_map(
        on_device, mesh=mesh, in_specs=in_specs, out_specs=out_specs, check_vma=False
    )
```

```python
import jax
import jax.numpy as jnp
from jax import lax
from jax.experimental import pallas as pl
from jax.experimental.pallas import tpu as pltpu
from jax.sharding import PartitionSpec as P

MESH = pl.DeviceIdType.MESH
BF16 = jnp.bfloat16
F32 = jnp.float32

NN = (((1,), (0,)), ((), ()))
NT = (((1,), (1,)), ((), ()))
TN = (((0,), (0,)), ((), ()))


def dot(a, b, dims):
    return lax.dot_general(a, b, dims, preferred_element_type=F32)


class Sems:
    def __init__(self, ref, size):
        self.ref, self.size, self.used = ref, size, 0

    def take(self):
        assert self.used < self.size
        self.used += 1
        return self.ref.at[self.used - 1]


N_SEND = 256
N_RECV = 224
GATHER = (0, 1, -1, 2)


def kernel(
    tok, gate_w, up_w, down_w, cot,
    out_ref, gtok_ref, ggate_ref, gup_ref, gdown_ref,
    down_t, xin, wts, wz, part_own, part_out, part_in, act, res, wgr,
    rxa0, rxa1, rxb0, rxb1, ry0, ry1, sy, fin, rza, rzb, sw, hw, gy, gz, rza2, rzb2,
    send_sems, recv_sems, hw_in, gy_in,
):
    i, x, o = lax.axis_index("inp"), lax.axis_index("wt"), lax.axis_index("out")
    h, c, l, z = i // 2, i % 2, o // 4, o % 4
    p = (h + l) % 2

    def dev(h, c, x, l, z):
        return {"inp": h * 2 + c, "wt": x, "out": l * 4 + z}

    def ring(v, d):
        return (v + d + 4) % 4

    x_to = [dev(h, c, ring(x, 1), l, z), dev(h, c, ring(x, -1), l, z)]
    z_to = [dev(h, c, x, l, ring(z, 1)), dev(h, c, x, l, ring(z, -1))]
    y_to = dev(1 - h, c, x, 1 - l, z)
    core_to = dev(h, 1 - c, x, l, z)
    WAYS = ((0, 1), (1, -1))

    sends = Sems(send_sems, N_SEND)
    recvs = Sems(recv_sems, N_RECV)
    pending = []

    def send(src, dst, sem, to):
        copy = pltpu.make_async_remote_copy(
            src, dst, sends.take(), sem, device_id=to, device_id_type=MESH
        )
        copy.start()
        pending.append(copy)

    def send_or_keep(src, dst, sem, to, mine):
        copy = pltpu.make_async_remote_copy(
            src, dst, sends.take(), sem, device_id=to, device_id_type=MESH
        )

        @pl.when(mine)
        def _():
            pltpu.make_async_copy(src, dst, sem).start()

        @pl.when(jnp.logical_not(mine))
        def _():
            copy.start()

        pending.append((copy, mine))

    def arrived(ref, sem):
        pltpu.make_async_copy(ref, ref, sem).wait()

    def rows(start, size):
        return pl.ds(pl.multiple_of(start, 64), size)

    def cols(start, size):
        return pl.ds(pl.multiple_of(start, 256), size)

    def take(n):
        return [recvs.take() for _ in range(n)]

    def add_into(ref, inc):
        ref[...] = (ref[...].astype(F32) + inc[...].astype(F32)).astype(BF16)

    barrier = pltpu.get_barrier_semaphore()
    met = 0
    for dl in range(2):
        for dz in range(4):
            for dc in range(2):
                if dl or dz or dc:
                    to = dev(h, (c + dc) % 2, x, (l + dl) % 2, ring(z, dz))
                    pl.semaphore_signal(barrier, inc=1, device_id=to, device_id_type=MESH)
                    met += 1
    for to in x_to + [y_to]:
        pl.semaphore_signal(barrier, inc=1, device_id=to, device_id_type=MESH)
        met += 1
    down_t[...] = down_w[...].T
    pl.semaphore_wait(barrier, met)

    source = [tok, cot]
    x_a2a = [take(4), take(4)]
    y0_in = take(4)
    y1_in = [take(4) for _ in range(4)]
    x_hop = {key: [[take(2), take(2)] for _ in range(4)] for key in ((1, 0), (0, 0), (0, 1))}
    w_in = [take(1), take(1), take(4)]
    z_hop = [[take(2), take(2)] for _ in range(3)]

    def x_slot(a, k, dx, other=0, start=0, size=128):
        hh = 1 - h if other else h
        return xin.at[a, ring(z, k), rows((ring(x, dx) * 2 + hh) * 128 + start, size), :]

    def scatter(a, dz):
        for dl in (1, 0):
            lt, zt = (l + dl) % 2, ring(z, dz)
            label = ((h + lt) % 2) * 4 + zt
            src = source[a].at[rows(label * 64, 64), :]
            dst = xin.at[a, z, rows((x * 2 + h) * 128 + c * 64, 64), :]
            to = dev(h, l, x, lt, zt)
            if dl or dz:
                send(src, dst, x_a2a[a][-dz % 4], to)
            else:
                send_or_keep(src, dst, x_a2a[a][0], to, c == l)

    def w_block(w, k, start=0, size=256):
        return wts.at[w, rows(ring(z, k) * 256 + start, size), :]

    def spread(w, src, k):
        dst = wts.at[w, rows(ring(z, k) * 256, 256), cols(c * 256, 256)]
        send(src, dst, w_in[w][k % 4], dev(h, l, x, 1 - l, z))
        send_or_keep(src, dst, w_in[w][k % 4], dev(h, l, x, l, z), c == l)

    def to_slot(k):
        arrived(x_slot(1, k, 0), x_a2a[1][k % 4])
        x_first(1, 0, k)
        y1_send(k, 0)
        arrived(x_slot(0, k, 0), x_a2a[0][k % 4])
        send(x_slot(0, k, 0), x_slot(0, k, 0), y0_in[k % 4], y_to)
        x_first(0, 0, k)

    def y1_send(k, dx):
        send(x_slot(1, k, dx), x_slot(1, k, dx), y1_in[k % 4][dx % 4], y_to)

    def x_first(a, other, k):
        for d in range(2):
            ref = x_slot(a, k, 0, other)
            send(ref, ref, x_hop[a, other][k % 4][0][d], x_to[d])

    def x_second(a, other, k):
        for d, dx in ((0, -1), (1, 1)):
            arrived(x_slot(a, k, dx, other), x_hop[a, other][k % 4][0][d])
            ref = x_slot(a, k, dx, other, 64 * d, 64)
            send(ref, ref, x_hop[a, other][k % 4][1][d], x_to[d])
            if a == 1:
                y1_send(k, dx)

    def x_last(a, other, k):
        for d in range(2):
            arrived(x_slot(a, k, 2, other, 64 * d, 64), x_hop[a, other][k % 4][1][d])
        if a == 1:
            y1_send(k, 2)

    def x_other(k):
        arrived(x_slot(0, k, 0, 1), y0_in[k % 4])
        x_first(0, 1, k)

    def z_first(w):
        arrived(w_block(w, 0), w_in[w][0])
        for d in range(2):
            send(w_block(w, 0), w_block(w, 0), z_hop[w][0][d], z_to[d])

    def z_second(w):
        for d, dz in ((0, -1), (1, 1)):
            arrived(w_block(w, dz), z_hop[w][0][d])
            ref = w_block(w, dz, 128 * d, 128)
            send(ref, ref, z_hop[w][1][d], z_to[d])

    def z_last(w):
        for d in range(2):
            arrived(w_block(w, 2, 128 * d, 128), z_hop[w][1][d])

    def d_first():
        for d in range(2):
            send(down_t, wz.at[z], z_hop[2][0][d], z_to[d])
        spread(2, down_t, 0)

    def d_second():
        for d, dz in ((0, -1), (1, 1)):
            at = ring(z, dz)
            arrived(wz.at[at], z_hop[2][0][d])
            ref = wz.at[at, rows(128 * d, 128), :]
            send(ref, ref, z_hop[2][1][d], z_to[d])
            spread(2, wz.at[at], dz)

    def d_last():
        at = ring(z, 2)
        for d in range(2):
            arrived(wz.at[at, rows(128 * d, 128), :], z_hop[2][1][d])
        spread(2, wz.at[at], 2)

    scatter(1, 0)
    scatter(0, 0)
    spread(0, gate_w, 0)
    for dz in (1, -1):
        scatter(1, dz)
    for dz in (1, -1):
        scatter(0, dz)
    spread(1, up_w, 0)
    scatter(1, 2)
    scatter(0, 2)
    d_first()

    to_slot(0)
    z_first(0)
    to_slot(1)
    to_slot(-1)
    z_first(1)
    x_second(1, 0, 0)
    x_second(0, 0, 0)
    x_other(0)
    to_slot(2)
    d_second()
    x_last(1, 0, 0)
    x_second(0, 1, 0)
    z_second(0)
    for k in (1, -1):
        x_second(1, 0, k)
        x_second(0, 0, k)
        x_other(k)
    z_second(1)
    for k in (1, -1):
        x_last(1, 0, k)
        x_second(0, 1, k)
    d_last()
    x_second(1, 0, 2)
    x_second(0, 0, 2)
    x_other(2)
    x_last(1, 0, 2)
    x_second(0, 1, 2)
    for k in GATHER:
        x_last(0, 0, k)
    z_last(0)
    z_last(1)
    for k in GATHER:
        arrived(w_block(2, k), w_in[2][k % 4])
        x_last(0, 1, k)

    p_in = take(4)
    a_in = take(4)

    def products(dx):
        for k in GATHER:
            arrived(x_slot(1, k, dx, 1), y1_in[k % 4][dx % 4])
        base = ring(x, dx) * 256
        for w in range(3):
            lhs = jnp.concatenate(
                [
                    jnp.concatenate(
                        [xin[w // 2, q, rows(base + hh * 128, 128), :] for q in range(4)], axis=1
                    )
                    for hh in (c, 1 - c)
                ],
                axis=0,
            )
            r = dot(lhs, wts[w], NN)
            part_own[dx % 4, w] = r[:128]
            part_out[dx % 4, w] = r[128:].astype(BF16)
        send(part_out.at[dx % 4], part_in.at[dx % 4], p_in[dx % 4], core_to)

    def activate(dx):
        g = dx % 4
        arrived(part_in.at[g], p_in[g])
        mine = ring(x, dx) * 256 + c * 128
        gate = part_own[g, 0] + part_in[g, 0].astype(F32)
        up = part_own[g, 1] + part_in[g, 1].astype(F32)
        back = part_own[g, 2] + part_in[g, 2].astype(F32)
        s = jax.nn.sigmoid(gate)
        silu = gate * s
        act[0, rows(mine, 128), :] = (back * up * (s * (1.0 + gate * (1.0 - s)))).astype(BF16)
        act[1, rows(mine, 128), :] = (back * silu).astype(BF16)
        act[2, rows(mine, 128), :] = (silu * up).astype(BF16)
        ref = act.at[:, rows(mine, 128), :]
        send(ref, ref, a_in[g], core_to)

    def act_ready(dx):
        theirs = ring(x, dx) * 256 + (1 - c) * 128
        arrived(act.at[:, rows(theirs, 128), :], a_in[dx % 4])

    products(0)
    products(1)
    activate(0)
    products(-1)
    activate(1)
    products(2)
    activate(-1)
    activate(2)

    ry0_in = take(4)
    ry1_in = [take(4) for _ in range(4)]
    rxa0_in, rxa1_in, rxb0_in, rxb1_in = ([take(2) for _ in range(4)] for _ in range(4))
    home_in = take(2)
    rza_in = [take(2) for _ in range(2)]
    rzb_in = [take(2) for _ in range(2)]
    rza2_in, rzb2_in = take(2), take(2)

    def r_group(k, dx, start=0, size=256):
        return res.at[0, ring(z, k), rows(ring(x, dx) * 256 + start, size), :]

    def r_slot(a, k, dx, other=0, start=0, size=128):
        hh = 1 - h if other else h
        return res.at[a, ring(z, k), rows((ring(x, dx) * 2 + hh) * 128 + start, size), :]

    def backward(k, dx):
        at = rows(ring(x, dx) * 256, 256)
        r = dot(act[0, at, :], w_block(0, k)[...], NT) + dot(act[1, at, :], w_block(1, k)[...], NT)
        res[1, ring(z, k), at, :] = r.astype(BF16)
        send(r_slot(1, k, dx, 1), ry1.at[k % 4, dx % 4], ry1_in[k % 4][dx % 4], y_to)
        r = dot(act[2, at, :], w_block(2, k)[...], NT)
        res[0, ring(z, k), at, :] = r.astype(BF16)

    def step1(k):
        backward(k, 2)
        for d in range(2):
            send(r_group(k, 2, 128 * d, 128), rxa0.at[k % 4, d], rxa0_in[k % 4][d], x_to[d])

    def step2(k):
        for d, dx in WAYS:
            arrived(rxa0.at[k % 4, d], rxa0_in[k % 4][d])
            add_into(r_group(k, dx, 128 * d, 128), rxa0.at[k % 4, d])
            send(r_group(k, dx), rxb0.at[k % 4, d], rxb0_in[k % 4][d], x_to[d])

    def y_sum(k, dx):
        arrived(ry1.at[k % 4, dx % 4], ry1_in[k % 4][dx % 4])
        add_into(r_slot(1, k, dx), ry1.at[k % 4, dx % 4])

    def slot1(k):
        y_sum(k, 2)
        for d in range(2):
            send(r_slot(1, k, 2, 0, 64 * d, 64), rxa1.at[k % 4, d], rxa1_in[k % 4][d], x_to[d])

    def slot2(k):
        for d, dx in WAYS:
            y_sum(k, dx)
            arrived(rxa1.at[k % 4, d], rxa1_in[k % 4][d])
            add_into(r_slot(1, k, dx, 0, 64 * d, 64), rxa1.at[k % 4, d])
            send(r_slot(1, k, dx), rxb1.at[k % 4, d], rxb1_in[k % 4][d], x_to[d])

    home = [out_ref, gtok_ref]

    def go_home(a, k):
        for dc in (1, 0):
            ct = (c + dc) % 2
            src = fin.at[a, k % 4, rows(ct * 64, 64), :]
            dst = home[a].at[rows((p * 4 + z) * 64, 64), :]
            to = dev(h, ct, x, c, ring(z, k))
            if k or dc:
                send(src, dst, home_in[a], to)
            else:
                send_or_keep(src, dst, home_in[a], to, c == l)

    def step3(k):
        for d in range(2):
            arrived(rxb0.at[k % 4, d], rxb0_in[k % 4][d])
        at = rows((1 - h) * 128, 128)
        sy[k % 4] = (
            r_slot(0, k, 0, 1)[...].astype(F32)
            + rxb0[k % 4, 0, at, :].astype(F32)
            + rxb0[k % 4, 1, at, :].astype(F32)
        ).astype(BF16)
        send(sy.at[k % 4], ry0.at[k % 4], ry0_in[k % 4], y_to)

    def step4(k):
        arrived(ry0.at[k % 4], ry0_in[k % 4])
        at = rows(h * 128, 128)
        fin[0, k % 4] = (
            r_slot(0, k, 0)[...].astype(F32)
            + rxb0[k % 4, 0, at, :].astype(F32)
            + rxb0[k % 4, 1, at, :].astype(F32)
            + ry0[k % 4].astype(F32)
        ).astype(BF16)
        go_home(0, k)

    def slot3(k):
        arrived(ry1.at[k % 4, 0], ry1_in[k % 4][0])
        for d in range(2):
            arrived(rxb1.at[k % 4, d], rxb1_in[k % 4][d])
        fin[1, k % 4] = (
            r_slot(1, k, 0)[...].astype(F32)
            + ry1[k % 4, 0].astype(F32)
            + rxb1[k % 4, 0].astype(F32)
            + rxb1[k % 4, 1].astype(F32)
        ).astype(BF16)
        go_home(1, k)

    def g_block(w, k, start=0, size=256):
        return wgr.at[w, rows(ring(z, k) * 256 + start, size), :]

    def weight_grad(w, k):
        r = dot(xin[w // 2, ring(z, k)], act[w], TN)
        g_block(w, k)[...] = r.astype(BF16)

    def grad1(w):
        weight_grad(w, 2)
        for d in range(2):
            send(g_block(w, 2, 128 * d, 128), rza.at[w, d], rza_in[w][d], z_to[d])

    def grad2(w):
        for d, dz in WAYS:
            weight_grad(w, dz)
            arrived(rza.at[w, d], rza_in[w][d])
            add_into(g_block(w, dz, 128 * d, 128), rza.at[w, d])
            send(g_block(w, dz), rzb.at[w, d], rzb_in[w][d], z_to[d])

    def grad3(w):
        weight_grad(w, 0)
        for d in range(2):
            arrived(rzb.at[w, d], rzb_in[w][d])
        sw[w] = (
            g_block(w, 0)[...].astype(F32) + rzb[w, 0].astype(F32) + rzb[w, 1].astype(F32)
        ).astype(BF16)
        for dc in (1, 0):
            ct = (c + dc) % 2
            src = sw.at[w, :, cols(ct * 256, 256)]
            to = dev(h, ct, x, c, z)
            if dc:
                send(src, hw.at[w, l], hw_in.at[w * 2 + l], to)
            else:
                send_or_keep(src, hw.at[w, l], hw_in.at[w * 2 + l], to, c == l)

    def down1(k):
        weight_grad(2, k)
        at = ring(z, k)
        for dc in (1, 0):
            ct = (c + dc) % 2
            src = wgr.at[2, rows(at * 256, 256), cols(ct * 256, 256)]
            sem = gy_in.at[(k % 4) * 2 + l]
            to = dev(h, ct, x, c, z)
            if dc:
                send(src, gy.at[l, at], sem, to)
            else:
                send_or_keep(src, gy.at[l, at], sem, to, c == l)

    def down_sum(k):
        at = ring(z, k)
        for ls in range(2):
            arrived(gy.at[ls, at], gy_in.at[(k % 4) * 2 + ls])
        gz[at] = (gy[0, at].astype(F32) + gy[1, at].astype(F32)).astype(BF16)

    def down2():
        down_sum(2)
        for d in range(2):
            ref = gz.at[ring(z, 2), rows(128 * d, 128), :]
            send(ref, rza2.at[d], rza2_in[d], z_to[d])

    def down3():
        for d, dz in WAYS:
            down_sum(dz)
            arrived(rza2.at[d], rza2_in[d])
            add_into(gz.at[ring(z, dz), rows(128 * d, 128), :], rza2.at[d])
            send(gz.at[ring(z, dz)], rzb2.at[d], rzb2_in[d], z_to[d])

    def down4():
        down_sum(0)
        for d in range(2):
            arrived(rzb2.at[d], rzb2_in[d])
        r = gz[z].astype(F32) + rzb2[0].astype(F32) + rzb2[1].astype(F32)
        gdown_ref[...] = r.T

    act_ready(0)
    act_ready(1)
    backward(2, 1)
    act_ready(-1)
    backward(2, -1)
    act_ready(2)
    step1(2)
    grad1(0)
    backward(2, 0)
    for k in (2, 1, -1, 0):
        down1(k)
    step1(1)
    slot1(2)
    step2(2)
    grad1(1)
    backward(1, 1)
    backward(1, -1)
    grad2(0)
    slot2(2)
    backward(1, 0)
    step1(-1)
    slot1(1)
    step3(2)
    step2(1)
    down2()
    backward(-1, 1)
    backward(-1, -1)
    slot3(2)
    slot2(1)
    backward(-1, 0)
    grad2(1)
    step4(2)
    step1(0)
    slot1(-1)
    step3(1)
    step2(-1)
    backward(0, 1)
    backward(0, -1)
    down3()
    slot3(1)
    grad3(0)
    slot2(-1)
    backward(0, 0)
    step4(1)
    slot1(0)
    step3(-1)
    step2(0)
    slot3(-1)
    grad3(1)
    slot2(0)
    step4(-1)
    step3(0)
    down4()
    slot3(0)
    step4(0)

    for w, ref in ((0, ggate_ref), (1, gup_ref)):
        for ls in range(2):
            arrived(hw.at[w, ls], hw_in.at[w * 2 + ls])
        ref[...] = hw[w, 0].astype(F32) + hw[w, 1].astype(F32)
    for a in (1, 0):
        arrived(home[a], home_in[a])

    for item in pending:
        if isinstance(item, tuple):
            copy, mine = item

            @pl.when(jnp.logical_not(mine))
            def _(copy=copy):
                copy.wait_send()
        else:
            item.wait_send()


def place(*refs):
    for src, dst in zip(refs[:5], refs[5:]):
        dst[...] = src[...]


def on_device(tokens, gate_weight, up_weight, down_weight, cotangent):
    vmem = pl.BlockSpec(memory_space=pltpu.VMEM)
    shapes = [jax.ShapeDtypeStruct((512, 256), BF16)] * 2
    shapes += [jax.ShapeDtypeStruct((256, 256), F32)] * 3
    results = pl.pallas_call(
        kernel,
        name="swiglu",
        out_shape=shapes,
        in_specs=[vmem] * 5,
        out_specs=[vmem] * 5,
        scratch_shapes=[
            pltpu.VMEM((256, 256), BF16),
            pltpu.VMEM((2, 4, 1024, 256), BF16),
            pltpu.VMEM((3, 1024, 512), BF16),
            pltpu.VMEM((4, 256, 256), BF16),
            pltpu.VMEM((4, 3, 128, 512), F32),
            pltpu.VMEM((4, 3, 128, 512), BF16),
            pltpu.VMEM((4, 3, 128, 512), BF16),
            pltpu.VMEM((3, 1024, 512), BF16),
            pltpu.VMEM((2, 4, 1024, 256), BF16),
            pltpu.VMEM((3, 1024, 512), BF16),
            pltpu.VMEM((4, 2, 128, 256), BF16),
            pltpu.VMEM((4, 2, 64, 256), BF16),
            pltpu.VMEM((4, 2, 256, 256), BF16),
            pltpu.VMEM((4, 2, 128, 256), BF16),
            pltpu.VMEM((4, 128, 256), BF16),
            pltpu.VMEM((4, 4, 128, 256), BF16),
            pltpu.VMEM((4, 128, 256), BF16),
            pltpu.VMEM((2, 4, 128, 256), BF16),
            pltpu.VMEM((2, 2, 128, 512), BF16),
            pltpu.VMEM((2, 2, 256, 512), BF16),
            pltpu.VMEM((2, 256, 512), BF16),
            pltpu.VMEM((2, 2, 256, 256), BF16),
            pltpu.VMEM((2, 4, 256, 256), BF16),
            pltpu.VMEM((4, 256, 256), BF16),
            pltpu.VMEM((2, 128, 256), BF16),
            pltpu.VMEM((2, 256, 256), BF16),
            pltpu.SemaphoreType.DMA((N_SEND,)),
            pltpu.SemaphoreType.DMA((N_RECV,)),
            pltpu.SemaphoreType.DMA((4,)),
            pltpu.SemaphoreType.DMA((8,)),
        ],
        compiler_params=pltpu.CompilerParams(
            collective_id=0, has_side_effects=True, vmem_limit_bytes=60 << 20
        ),
        cost_estimate=pl.CostEstimate(
            flops=9 * 2 * 1024 * 1024 * 512, bytes_accessed=3 << 20, transcendentals=1024 * 256
        ),
    )(
        tokens.reshape(512, 256),
        gate_weight,
        up_weight,
        down_weight,
        cotangent.reshape(512, 256),
    )
    output, grad_tokens, grad_gate, grad_up, grad_down = pl.pallas_call(
        place, name="place", out_shape=shapes, in_specs=[vmem] * 5, out_specs=[vmem] * 5
    )(*results)
    return (
        output.reshape(2, 256, 256),
        grad_tokens.reshape(2, 256, 256),
        grad_gate,
        grad_up,
        grad_down,
    )


def solution(mesh):
    in_specs = (
        P(None, ("inp", "wt"), "out"),
        P("out", ("wt", "inp")),
        P("out", ("wt", "inp")),
        P(("wt", "inp"), "out"),
        P(None, ("inp", "wt"), "out"),
    )
    out_specs = (
        P(None, ("inp", "wt"), "out"),
        P(None, ("inp", "wt"), "out"),
        P("out", ("wt", "inp")),
        P("out", ("wt", "inp")),
        P(("wt", "inp"), "out"),
    )
    return jax.shard_map(
        on_device, mesh=mesh, in_specs=in_specs, out_specs=out_specs, check_vma=False
    )
```

```python
import jax
import jax.numpy as jnp
from jax import lax
from jax.experimental import pallas as pl
from jax.experimental.pallas import tpu as pltpu
from jax.sharding import PartitionSpec as P

MESH = pl.DeviceIdType.MESH
BF16 = jnp.bfloat16
F32 = jnp.float32

NN = (((1,), (0,)), ((), ()))
NT = (((1,), (1,)), ((), ()))
TN = (((0,), (0,)), ((), ()))


def dot(a, b, dims):
    return lax.dot_general(a, b, dims, preferred_element_type=F32)


class Sems:
    def __init__(self, ref, size):
        self.ref, self.size, self.used = ref, size, 0

    def take(self, n=None):
        start = self.used
        self.used += n or 1
        assert self.used <= self.size
        return [self.ref.at[start + j] for j in range(n)] if n else self.ref.at[start]


N_SEND = 80
N_RECV = 150
GATHER = (0, 1, 3, 2)
FROM = ((0, 3), (1, 1))
TO = ((0, 1), (1, 3))


def kernel(
    tok, gate_w, up_w, down_w, cot,
    out_ref, gtok_ref, ggate_ref, gup_ref, gdown_ref,
    down_in, xin, wts, part, act, res, wgr, wgo, wgi,
    rxa0, rxa1, rxb0, rxb1, ry0, ry1, sy, fin, rza, rzb, gy, gl, rza2, rzb2, gy2,
    send_sems, recv_sems, own_sem,
):
    i, x, o = lax.axis_index("inp"), lax.axis_index("wt"), lax.axis_index("out")
    h, c, l, z = i // 2, i % 2, o // 4, o % 4
    p = (h + l) % 2

    def dev(h, c, x, l, z):
        return {"inp": h * 2 + c, "wt": x, "out": l * 4 + z}

    def ring(v, d):
        return (v + d) % 4

    x_to = [dev(h, c, ring(x, 1), l, z), dev(h, c, ring(x, 3), l, z)]
    z_to = [dev(h, c, x, l, ring(z, 1)), dev(h, c, x, l, ring(z, 3))]
    y_to = dev(1 - h, c, x, 1 - l, z)
    l_to = dev(h, c, x, 1 - l, z)
    core_to = dev(h, 1 - c, x, l, z)

    recvs = Sems(recv_sems, N_RECV)
    take = recvs.take
    pool = [None] * N_SEND
    count = [0]

    def send(src, dst, sem, to):
        n = count[0] % N_SEND
        count[0] += 1
        if pool[n] is not None:
            pool[n].wait_send()
        pool[n] = pltpu.make_async_remote_copy(
            src, dst, send_sems.at[n], sem, device_id=to, device_id_type=MESH
        )
        pool[n].start()

    def keep(src, dst, sem):
        pltpu.make_async_copy(src, dst, sem).start()

    def arrived(ref, sem):
        pltpu.make_async_copy(ref, ref, sem).wait()

    def rows(start, size):
        return pl.ds(pl.multiple_of(start, 64), size)

    def add_into(ref, inc):
        ref[...] = (ref[...].astype(F32) + inc[...].astype(F32)).astype(BF16)

    fetch = pltpu.make_async_copy(down_w, down_in, own_sem)
    fetch.start()
    barrier = pltpu.get_barrier_semaphore()
    partners = [dev(h, c, x, (l + dl) % 2, ring(z, dz)) for dl in range(2) for dz in range(4)][1:]
    partners += x_to + [y_to, core_to]
    for to in partners:
        pl.semaphore_signal(barrier, inc=1, device_id=to, device_id_type=MESH)
    fetch.wait()
    wts[2, c, l, 0] = down_in[...].T
    pl.semaphore_wait(barrier, len(partners))

    source = [tok, cot]
    a2a_in = [take(4), take(4)]
    x_hop = {(a, r, k): [take(2), take()] for k in range(4) for a, r in ((1, 0), (0, 0), (0, 1))}
    y0_in, y1_in = take(4), take(4)
    w_in = [take(1), take(1), take(4)]
    z_hop = [[take(2), take()] for _ in range(3)]
    pass_in = [take(4) for _ in range(3)]

    def x_slot(a, k, g, r=0, start=0, size=64):
        return xin.at[a, :, k, r, pl.ds(g * 64 + start, size), :]

    def scatter(a, dz):
        k = -dz % 4
        for dl in (1, 0):
            lt, zt = (l + dl) % 2, ring(z, dz)
            src = source[a].at[rows((((h + lt) % 2) * 4 + zt) * 64, 64), :]
            dst = xin.at[a, l, k, 0, pl.ds(0, 64), :]
            if dl or dz:
                send(src, dst, a2a_in[a][k], dev(h, c, x, lt, zt))
            else:
                keep(src, dst, a2a_in[a][k])

    def x_first(a, r, k):
        for d, g in FROM:
            send(x_slot(a, k, 0, r), x_slot(a, k, g, r), x_hop[a, r, k][0][d], x_to[d])

    def y1_send(k, g):
        send(x_slot(1, k, g), x_slot(1, k, g, 1), y1_in[k], y_to)

    def cot_in(k):
        arrived(x_slot(1, k, 0), a2a_in[1][k])
        x_first(1, 0, k)
        y1_send(k, 0)

    def tok_in(k):
        arrived(x_slot(0, k, 0), a2a_in[0][k])
        send(x_slot(0, k, 0), x_slot(0, k, 0, 1), y0_in[k], y_to)
        x_first(0, 0, k)

    def tok_other(k):
        arrived(x_slot(0, k, 0, 1), y0_in[k])
        x_first(0, 1, k)

    def x_second(a, r, k, d):
        g = FROM[d][1]
        arrived(x_slot(a, k, g, r), x_hop[a, r, k][0][d])
        half = (32 * d, 32)
        send(x_slot(a, k, g, r, *half), x_slot(a, k, 2, r, *half), x_hop[a, r, k][1], x_to[d])
        if a == 1:
            y1_send(k, g)

    def x_last(k):
        arrived(x_slot(1, k, 2), x_hop[1, 0, k][1])
        y1_send(k, 2)

    def gathered(k):
        for r in range(2):
            arrived(x_slot(0, k, 2, r), x_hop[0, r, k][1])
        arrived(xin.at[1, :, k, 1], y1_in[k])

    def w_blocks(w, k, start=0, size=256):
        return wts.at[w, c, :, k, pl.ds(start, size), :]

    def w_own(w):
        src, dst = [gate_w, up_w][w], wts.at[w, c, l, 0]
        send(src, dst, w_in[w][0], l_to)
        keep(src, dst, w_in[w][0])

    def w_pass(w, k):
        send(w_blocks(w, k), w_blocks(w, k), pass_in[w][k], core_to)

    def z_first(w):
        arrived(w_blocks(w, 0), w_in[w][0])
        for d, k in FROM:
            send(w_blocks(w, 0), w_blocks(w, k), z_hop[w][0][d], z_to[d])
        w_pass(w, 0)

    def z_second(w, d):
        k = FROM[d][1]
        arrived(w_blocks(w, k), z_hop[w][0][d])
        half = (128 * d, 128)
        send(w_blocks(w, k, *half), w_blocks(w, 2, *half), z_hop[w][1], z_to[d])
        w_pass(w, k)

    def z_last(w):
        arrived(w_blocks(w, 2), z_hop[w][1])
        w_pass(w, 2)

    def d_block(k, start=0, size=256):
        return wts.at[2, c, l, k, pl.ds(start, size), :]

    def d_first():
        for d, k in FROM:
            send(d_block(0), d_block(k), z_hop[2][0][d], z_to[d])
        send(d_block(0), d_block(0), w_in[2][0], l_to)

    def d_second(d):
        k = FROM[d][1]
        arrived(d_block(k), z_hop[2][0][d])
        half = (128 * d, 128)
        send(d_block(k, *half), d_block(2, *half), z_hop[2][1], z_to[d])
        send(d_block(k), d_block(k), w_in[2][k], l_to)

    def d_last():
        arrived(d_block(2), z_hop[2][1])
        send(d_block(2), d_block(2), w_in[2][2], l_to)

    def d_pass(k):
        arrived(wts.at[2, c, 1 - l, k], w_in[2][k])
        w_pass(2, k)

    def weight_ready(w, k):
        arrived(wts.at[w, 1 - c, :, k], pass_in[w][k])

    early = [(q, k) for q in range(2) for k in GATHER[:3]]
    late = [(q, GATHER[3]) for q in range(2)]

    def product(w, f, blocks):
        lhs = jnp.concatenate([xin[w // 2, q, k].reshape(512, 256) for q, k in blocks], axis=1)
        rhs = jnp.concatenate([wts[w, f, q, k] for q, k in blocks], axis=0)
        return dot(lhs, rhs, NN)

    def products(w):
        for f in range(2):
            part[w, f] = product(w, f, early)

    def activate(f):
        gate = part[0, f] + product(0, f, late)
        up = part[1, f] + product(1, f, late)
        back = part[2, f] + product(2, f, late)
        s = jax.nn.sigmoid(gate)
        silu = gate * s
        act[0, f] = (back * up * (s * (1.0 + gate * (1.0 - s)))).astype(BF16)
        act[1, f] = (back * silu).astype(BF16)
        act[2, f] = (silu * up).astype(BF16)

    ry0_in, ry1_in, rxb0_in, rxb1_in = (take(4) for _ in range(4))
    rxa0_in, rxa1_in = ([take(2) for _ in range(4)] for _ in range(2))
    home_in = take(2)

    def backward(w, q, k):
        lhs = jnp.concatenate([act[w, 0], act[w, 1]], axis=1)
        return dot(lhs, jnp.concatenate([wts[w, 0, q, k], wts[w, 1, q, k]], axis=1), NT)

    def slot0(k):
        for q in range(2):
            r = backward(0, q, k) + backward(1, q, k)
            res[1, q, k] = r.astype(BF16).reshape(2, 256, 256)
        send(res.at[1, :, k, 1], ry1.at[:, k], ry1_in[k], y_to)

    def group(k, g):
        return res.at[0, :, k, :, pl.ds(g * 64, 64), :]

    def half_group(k, g, r):
        return res.at[0, :, k, r, pl.ds(g * 64, 64), :]

    def slot(k, g, start=0, size=64):
        return res.at[1, :, k, 0, pl.ds(g * 64 + start, size), :]

    def step1(k):
        for q in range(2):
            res[0, q, k] = backward(2, q, k).astype(BF16).reshape(2, 256, 256)
        for d in range(2):
            send(half_group(k, 2, d), rxa0.at[d, :, k], rxa0_in[k][d], x_to[d])

    def step2(k, d):
        g = TO[d][1]
        arrived(rxa0.at[d, :, k], rxa0_in[k][d])
        add_into(half_group(k, g, d), rxa0.at[d, :, k])
        send(group(k, g), rxb0.at[d, :, k], rxb0_in[k], x_to[d])

    def step3(k):
        arrived(rxb0.at[:, :, k], rxb0_in[k])
        sy[:, k] = (
            res[0, :, k, 1, 0:64, :].astype(F32)
            + rxb0[0, :, k, 1].astype(F32)
            + rxb0[1, :, k, 1].astype(F32)
        ).astype(BF16)
        send(sy.at[:, k], ry0.at[:, k], ry0_in[k], y_to)

    home = [out_ref, gtok_ref]

    def go_home(a, k):
        dst = home[a].at[rows((p * 4 + z) * 64, 64), :]
        for dl in (1, 0):
            q = (l + dl) % 2
            if dl or k:
                send(fin.at[a, q, k], dst, home_in[a], dev(h, c, x, q, ring(z, k)))
            else:
                keep(fin.at[a, q, k], dst, home_in[a])

    def step4(k):
        arrived(ry0.at[:, k], ry0_in[k])
        fin[0, :, k] = (
            res[0, :, k, 0, 0:64, :].astype(F32)
            + rxb0[0, :, k, 0].astype(F32)
            + rxb0[1, :, k, 0].astype(F32)
            + ry0[:, k].astype(F32)
        ).astype(BF16)
        go_home(0, k)

    def slot1(k):
        arrived(ry1.at[:, k], ry1_in[k])
        add_into(res.at[1, :, k, 0], ry1.at[:, k])
        for d in range(2):
            send(slot(k, 2, 32 * d, 32), rxa1.at[d, :, k], rxa1_in[k][d], x_to[d])

    def slot2(k, d):
        g = TO[d][1]
        arrived(rxa1.at[d, :, k], rxa1_in[k][d])
        add_into(slot(k, g, 32 * d, 32), rxa1.at[d, :, k])
        send(slot(k, g), rxb1.at[d, :, k], rxb1_in[k], x_to[d])

    def slot3(k):
        arrived(rxb1.at[:, :, k], rxb1_in[k])
        fin[1, :, k] = (
            res[1, :, k, 0, 0:64, :].astype(F32)
            + rxb1[0, :, k].astype(F32)
            + rxb1[1, :, k].astype(F32)
        ).astype(BF16)
        go_home(1, k)

    sum_in = [take(4) for _ in range(3)]
    rza_in = [take(2) for _ in range(2)]
    rzb_in, gy_in = take(2), take(2)
    rza2_in, rzb2_in, gy2_in = take(2), take(), take(4)

    def grad0(w, k):
        for q in range(2):
            lhs = xin[w // 2, q, k].reshape(512, 256)
            wgo[w, q, k] = dot(lhs, act[w, 1 - c], TN).astype(BF16)
        send(wgo.at[w, :, k], wgi.at[w, :, k], sum_in[w][k], core_to)
        for q in range(2):
            lhs = xin[w // 2, q, k].reshape(512, 256)
            wgr[w, q, k] = dot(lhs, act[w, c], TN).astype(BF16)

    def both(w, k):
        arrived(wgi.at[w, :, k], sum_in[w][k])
        add_into(wgr.at[w, :, k], wgi.at[w, :, k])

    def grad1(w):
        both(w, 2)
        for d in range(2):
            send(wgr.at[w, :, 2, pl.ds(128 * d, 128), :], rza.at[w, d], rza_in[w][d], z_to[d])

    def grad2(w, d):
        k = TO[d][1]
        both(w, k)
        arrived(rza.at[w, d], rza_in[w][d])
        add_into(wgr.at[w, :, k, pl.ds(128 * d, 128), :], rza.at[w, d])
        send(wgr.at[w, :, k], rzb.at[w, d], rzb_in[w], z_to[d])

    def grad3(w):
        both(w, 0)
        arrived(rzb.at[w], rzb_in[w])
        gl[w] = (
            wgr[w, :, 0].astype(F32) + rzb[w, 0].astype(F32) + rzb[w, 1].astype(F32)
        ).astype(BF16)
        send(gl.at[w, 1 - l], gy.at[w], gy_in[w], l_to)

    def grad4(w):
        arrived(gy.at[w], gy_in[w])
        [ggate_ref, gup_ref][w][...] = gl[w, l].astype(F32) + gy[w].astype(F32)

    def down1(k):
        both(2, k)
        send(wgr.at[2, 1 - l, k], gy2.at[k], gy2_in[k], l_to)

    def down_sum(k):
        arrived(gy2.at[k], gy2_in[k])
        add_into(wgr.at[2, l, k], gy2.at[k])

    def down2():
        down_sum(2)
        for d in range(2):
            send(wgr.at[2, l, 2, pl.ds(128 * d, 128), :], rza2.at[d], rza2_in[d], z_to[d])

    def down3(d):
        k = TO[d][1]
        down_sum(k)
        arrived(rza2.at[d], rza2_in[d])
        add_into(wgr.at[2, l, k, pl.ds(128 * d, 128), :], rza2.at[d])
        send(wgr.at[2, l, k], rzb2.at[d], rzb2_in, z_to[d])

    def down4():
        down_sum(0)
        arrived(rzb2, rzb2_in)
        r = wgr[2, l, 0].astype(F32) + rzb2[0].astype(F32) + rzb2[1].astype(F32)
        gdown_ref[...] = r.T

    def finish():
        for a in (1, 0):
            arrived(home[a], home_in[a])

    for step, *args in (
        (scatter, 1, 0), (scatter, 0, 0), (scatter, 1, 1), (scatter, 1, 3), (scatter, 0, 1), (scatter, 0, 3),
        (w_own, 0), (w_own, 1), (scatter, 1, 2), (scatter, 0, 2), (d_first,), (cot_in, 0), (tok_in, 0),
        (cot_in, 3), (cot_in, 1), (tok_in, 3), (tok_in, 1), (x_second, 1, 0, 0, 0), (x_second, 1, 0, 0, 1),
        (x_second, 0, 0, 0, 0), (x_second, 0, 0, 0, 1), (tok_other, 0), (z_first, 0), (x_second, 1, 0, 3, 0),
        (x_second, 1, 0, 3, 1), (d_second, 0), (x_second, 1, 0, 1, 0), (x_second, 1, 0, 1, 1), (d_second, 1),
        (z_first, 1), (x_second, 0, 0, 3, 0), (x_second, 0, 0, 3, 1), (tok_other, 3), (weight_ready, 0, 0),
        (cot_in, 2), (tok_in, 2), (x_second, 0, 0, 1, 0), (x_second, 0, 0, 1, 1), (tok_other, 1), (x_last, 0),
        (weight_ready, 1, 0), (d_pass, 0), (x_second, 0, 1, 0, 0), (x_second, 0, 1, 0, 1), (z_second, 0, 0),
        (x_last, 3), (z_second, 0, 1), (x_last, 1), (d_last,), (d_pass, 3), (weight_ready, 2, 0),
        (x_second, 0, 1, 3, 0), (x_second, 0, 1, 3, 1), (weight_ready, 0, 3), (weight_ready, 0, 1),
        (x_second, 1, 0, 2, 0), (x_second, 1, 0, 2, 1), (d_pass, 1), (weight_ready, 2, 3),
        (x_second, 0, 0, 2, 0), (x_second, 0, 0, 2, 1), (z_second, 1, 0), (z_second, 1, 1), (d_pass, 2),
        (x_second, 0, 1, 1, 0), (x_second, 0, 1, 1, 1), (tok_other, 2), (weight_ready, 2, 1), (gathered, 0),
        (x_last, 2), (z_last, 0), (weight_ready, 1, 3), (gathered, 3), (weight_ready, 1, 1),
        (weight_ready, 2, 2), (gathered, 1), (products, 0), (x_second, 0, 1, 2, 0), (x_second, 0, 1, 2, 1),
        (z_last, 1), (weight_ready, 0, 2), (products, 1), (products, 2), (gathered, 2), (weight_ready, 1, 2),
        (activate, 0), (activate, 1), (slot0, 2), (step1, 2), (grad0, 0, 2), (slot0, 1), (step1, 1),
        (slot0, 3), (step1, 3), (grad0, 1, 2), (grad1, 0), (step2, 2, 0), (step2, 2, 1), (grad0, 2, 2),
        (grad0, 0, 1), (grad0, 0, 3), (step2, 1, 0), (step2, 1, 1), (grad0, 1, 1), (grad0, 2, 1), (grad1, 1),
        (step2, 3, 0), (step2, 3, 1), (grad0, 1, 3), (slot1, 2), (down1, 2), (slot0, 0), (grad2, 0, 0),
        (grad2, 0, 1), (step1, 0), (step3, 2), (down1, 1), (grad0, 2, 3), (grad0, 0, 0), (grad0, 1, 0),
        (grad0, 2, 0), (grad2, 1, 0), (step3, 1), (grad2, 1, 1), (slot1, 1), (down2,), (down1, 3), (step3, 3),
        (down1, 0), (slot2, 2, 0), (slot2, 2, 1), (step2, 0, 0), (step2, 0, 1), (grad3, 0), (slot2, 1, 0),
        (slot2, 1, 1), (slot1, 3), (slot3, 2), (step3, 0), (grad3, 1), (slot1, 0), (slot3, 1), (down3, 0),
        (down3, 1), (slot2, 3, 0), (slot2, 3, 1), (grad4, 0), (step4, 2), (step4, 1), (slot2, 0, 0),
        (slot2, 0, 1), (step4, 3), (grad4, 1), (slot3, 3), (step4, 0), (down4,), (slot3, 0), (finish,),
    ):
        step(*args)
    for copy in pool:
        if copy is not None:
            copy.wait_send()


def place(*refs):
    held, sems = refs[10:15], refs[15]
    come = [pltpu.make_async_copy(refs[n], held[n], sems.at[n]) for n in range(5)]
    go = [pltpu.make_async_copy(held[n], refs[5 + n], sems.at[5 + n]) for n in range(5)]
    for copy in come:
        copy.start()
    for first, then in zip(come, go):
        first.wait()
        then.start()
    for copy in go:
        copy.wait()


def on_device(tokens, gate_weight, up_weight, down_weight, cotangent):
    vmem = pl.BlockSpec(memory_space=pltpu.VMEM)
    anywhere = pl.BlockSpec(memory_space=pl.ANY)
    shapes = [jax.ShapeDtypeStruct((512, 256), BF16)] * 2
    shapes += [jax.ShapeDtypeStruct((256, 256), F32)] * 3
    results = pl.pallas_call(
        kernel,
        name="swiglu",
        out_shape=shapes,
        in_specs=[anywhere] * 5,
        out_specs=[anywhere] * 2 + [vmem] * 3,
        scratch_shapes=[
            pltpu.VMEM((256, 256), BF16),
            pltpu.VMEM((2, 2, 4, 2, 256, 256), BF16),
            pltpu.VMEM((3, 2, 2, 4, 256, 256), BF16),
            pltpu.VMEM((3, 2, 512, 256), F32),
            pltpu.VMEM((3, 2, 512, 256), BF16),
            pltpu.VMEM((2, 2, 4, 2, 256, 256), BF16),
            pltpu.VMEM((3, 2, 4, 256, 256), BF16),
            pltpu.VMEM((3, 2, 4, 256, 256), BF16),
            pltpu.VMEM((3, 2, 4, 256, 256), BF16),
            pltpu.VMEM((2, 2, 4, 64, 256), BF16),
            pltpu.VMEM((2, 2, 4, 32, 256), BF16),
            pltpu.VMEM((2, 2, 4, 2, 64, 256), BF16),
            pltpu.VMEM((2, 2, 4, 64, 256), BF16),
            pltpu.VMEM((2, 4, 64, 256), BF16),
            pltpu.VMEM((2, 4, 256, 256), BF16),
            pltpu.VMEM((2, 4, 64, 256), BF16),
            pltpu.VMEM((2, 2, 4, 64, 256), BF16),
            pltpu.VMEM((2, 2, 2, 128, 256), BF16),
            pltpu.VMEM((2, 2, 2, 256, 256), BF16),
            pltpu.VMEM((2, 256, 256), BF16),
            pltpu.VMEM((2, 2, 256, 256), BF16),
            pltpu.VMEM((2, 128, 256), BF16),
            pltpu.VMEM((2, 256, 256), BF16),
            pltpu.VMEM((4, 256, 256), BF16),
            pltpu.SemaphoreType.DMA((N_SEND,)),
            pltpu.SemaphoreType.DMA((N_RECV,)),
            pltpu.SemaphoreType.DMA,
        ],
        compiler_params=pltpu.CompilerParams(
            collective_id=0, has_side_effects=True, vmem_limit_bytes=60 << 20
        ),
        cost_estimate=pl.CostEstimate(
            flops=9 * 2 * 1024 * 1024 * 512, bytes_accessed=3 << 20, transcendentals=1024 * 256
        ),
    )(
        tokens.reshape(512, 256),
        gate_weight,
        up_weight,
        down_weight,
        cotangent.reshape(512, 256),
    )
    output, grad_tokens, grad_gate, grad_up, grad_down = pl.pallas_call(
        place,
        name="place",
        out_shape=shapes,
        in_specs=[anywhere] * 5,
        out_specs=[anywhere] * 5,
        scratch_shapes=[pltpu.VMEM(s.shape, s.dtype) for s in shapes]
        + [pltpu.SemaphoreType.DMA((10,))],
    )(*results)
    return (
        output.reshape(2, 256, 256),
        grad_tokens.reshape(2, 256, 256),
        grad_gate,
        grad_up,
        grad_down,
    )


def solution(mesh):
    in_specs = (
        P(None, ("inp", "wt"), "out"),
        P("out", ("wt", "inp")),
        P("out", ("wt", "inp")),
        P(("wt", "inp"), "out"),
        P(None, ("inp", "wt"), "out"),
    )
    out_specs = (
        P(None, ("inp", "wt"), "out"),
        P(None, ("inp", "wt"), "out"),
        P("out", ("wt", "inp")),
        P("out", ("wt", "inp")),
        P(("wt", "inp"), "out"),
    )
    return jax.shard_map(
        on_device, mesh=mesh, in_specs=in_specs, out_specs=out_specs, check_vma=False
    )
```

```python
import jax
import jax.numpy as jnp
from jax import lax
from jax.experimental import pallas as pl
from jax.experimental.pallas import tpu as pltpu
from jax.sharding import PartitionSpec as P

MESH = pl.DeviceIdType.MESH
BF16 = jnp.bfloat16
F32 = jnp.float32

NN = (((1,), (0,)), ((), ()))
NT = (((1,), (1,)), ((), ()))
TN = (((0,), (0,)), ((), ()))


def dot(a, b, dims):
    return lax.dot_general(a, b, dims, preferred_element_type=F32)


class Sems:
    def __init__(self, ref, size):
        self.ref, self.size, self.used = ref, size, 0

    def take(self, n=None):
        start = self.used
        self.used += n or 1
        assert self.used <= self.size
        return [self.ref.at[start + j] for j in range(n)] if n else self.ref.at[start]


N_SEND = 80
N_RECV = 190
GATHER = (0, 1, 3, 2)
CROSS_IN = (0,)
CROSS_OUT = (2,)
FROM = ((0, 3), (1, 1))
TO = ((0, 1), (1, 3))


def ways_in(k):
    return ((0, 0), (0, 1), (1, 0), (1, 1)) if k in CROSS_IN else ((0, 0), (0, 1), (1, 0))


def kernel(
    tok, gate_w, up_w, down_w, cot,
    out_ref, gtok_ref, ggate_ref, gup_ref, gdown_ref,
    down_in, xin, wts, part, act, res, wgr, wgo, wgi,
    rxa0, rxa1, rxb0, rxb1, ry0, ry1, sy, fin, rza, rzb, gy, gl, rza2, rzb2, gy2,
    send_sems, recv_sems, own_sem,
):
    i, x, o = lax.axis_index("inp"), lax.axis_index("wt"), lax.axis_index("out")
    h, c, l, z = i // 2, i % 2, o // 4, o % 4
    p = (h + l) % 2

    def dev(h, c, x, l, z):
        return {"inp": h * 2 + c, "wt": x, "out": l * 4 + z}

    def ring(v, d):
        return (v + d) % 4

    x_to = [dev(h, c, ring(x, 1), l, z), dev(h, c, ring(x, 3), l, z)]
    z_to = [dev(h, c, x, l, ring(z, 1)), dev(h, c, x, l, ring(z, 3))]
    y_to = dev(1 - h, c, x, 1 - l, z)
    l_to = dev(h, c, x, 1 - l, z)
    core_to = dev(h, 1 - c, x, l, z)

    recvs = Sems(recv_sems, N_RECV)
    take = recvs.take
    pool = [None] * N_SEND
    count = [0]

    def send(src, dst, sem, to):
        n = count[0] % N_SEND
        count[0] += 1
        if pool[n] is not None:
            pool[n].wait_send()
        pool[n] = pltpu.make_async_remote_copy(
            src, dst, send_sems.at[n], sem, device_id=to, device_id_type=MESH
        )
        pool[n].start()

    def keep(src, dst, sem):
        pltpu.make_async_copy(src, dst, sem).start()

    def arrived(ref, sem):
        pltpu.make_async_copy(ref, ref, sem).wait()

    def rows(start, size):
        return pl.ds(pl.multiple_of(start, 64), size)

    def add_into(ref, inc):
        ref[...] = (ref[...].astype(F32) + inc[...].astype(F32)).astype(BF16)

    fetch = pltpu.make_async_copy(down_w, down_in, own_sem)
    fetch.start()
    barrier = pltpu.get_barrier_semaphore()
    partners = [dev(h, c, x, (l + dl) % 2, ring(z, dz)) for dl in range(2) for dz in range(4)][1:]
    partners += x_to + [y_to, core_to]
    for to in partners:
        pl.semaphore_signal(barrier, inc=1, device_id=to, device_id_type=MESH)
    fetch.wait()
    wts[2, c, l, 0] = down_in[...].T
    pl.semaphore_wait(barrier, len(partners))

    source = [tok, cot]
    a2a_in = [take(4), take(4)]
    x_hop = {(a, r, k): [take(2), take()] for k in range(4) for a, r in ways_in(k)}
    y0_in, y1_in = [take(4), [take() if k in CROSS_IN else None for k in range(4)]], take(4)
    w_in = [take(1), take(1), take(4)]
    z_hop = [[take(2), take()] for _ in range(3)]
    pass_in = [take(4) for _ in range(3)]

    def x_slot(a, k, g, r=0, start=0, size=64):
        return xin.at[a, :, k, r, pl.ds(g * 64 + start, size), :]

    def scatter(a, dz):
        k = -dz % 4
        for dl in (1, 0):
            lt, zt = (l + dl) % 2, ring(z, dz)
            src = source[a].at[rows((((h + lt) % 2) * 4 + zt) * 64, 64), :]
            dst = xin.at[a, l, k, 0, pl.ds(0, 64), :]
            if dl or dz:
                send(src, dst, a2a_in[a][k], dev(h, c, x, lt, zt))
            else:
                keep(src, dst, a2a_in[a][k])

    def y_first(a, k):
        return a == 0 or k in CROSS_IN

    def early(a):
        src = source[a].at[rows((p * 4 + z) * 64, 64), :]
        for d, g in FROM:
            dst = xin.at[a, l, 0, 0, pl.ds(g * 64, 64), :]
            send(src, dst, x_hop[a, 0, 0][0][d], x_to[d])
        sem = y0_in[a][0] if y_first(a, 0) else y1_in[0]
        send(src, xin.at[a, l, 0, 1, pl.ds(0, 64), :], sem, y_to)

    def x_first(a, r, k):
        for d, g in FROM:
            src, dst = x_slot(a, k, 0, r), x_slot(a, k, g, r)
            if r == 0 and k == 0:
                src = xin.at[a, 1 - l, 0, 0, pl.ds(0, 64), :]
                dst = xin.at[a, 1 - l, 0, 0, pl.ds(g * 64, 64), :]
            send(src, dst, x_hop[a, r, k][0][d], x_to[d])

    def y_own(a, k, sem):
        src, dst = x_slot(a, k, 0), x_slot(a, k, 0, 1)
        if k == 0:
            src = xin.at[a, 1 - l, 0, 0, pl.ds(0, 64), :]
            dst = xin.at[a, 1 - l, 0, 1, pl.ds(0, 64), :]
        send(src, dst, sem, y_to)

    def y1_send(k, g):
        send(x_slot(1, k, g), x_slot(1, k, g, 1), y1_in[k], y_to)

    def x_in(a, k):
        arrived(x_slot(a, k, 0), a2a_in[a][k])
        if y_first(a, k):
            y_own(a, k, y0_in[a][k])
            x_first(a, 0, k)
        else:
            x_first(a, 0, k)
            y_own(a, k, y1_in[k])

    def x_other(a, k):
        arrived(x_slot(a, k, 0, 1), y0_in[a][k])
        x_first(a, 1, k)

    def x_second(a, r, k, d):
        g = FROM[d][1]
        arrived(x_slot(a, k, g, r), x_hop[a, r, k][0][d])
        half = (32 * d, 32)
        send(x_slot(a, k, g, r, *half), x_slot(a, k, 2, r, *half), x_hop[a, r, k][1], x_to[d])
        if not y_first(a, k):
            y1_send(k, g)

    def x_last(k):
        arrived(x_slot(1, k, 2), x_hop[1, 0, k][1])
        y1_send(k, 2)

    def gathered(k):
        for a in range(2):
            if y_first(a, k):
                for r in range(2):
                    arrived(x_slot(a, k, 2, r), x_hop[a, r, k][1])
            else:
                arrived(xin.at[a, :, k, 1], y1_in[k])

    def w_blocks(w, k, start=0, size=256):
        return wts.at[w, c, :, k, pl.ds(start, size), :]

    def w_own(w):
        src, dst = [gate_w, up_w][w], wts.at[w, c, l, 0]
        send(src, dst, w_in[w][0], l_to)
        keep(src, dst, w_in[w][0])

    def w_pass(w, k):
        send(w_blocks(w, k), w_blocks(w, k), pass_in[w][k], core_to)

    def z_first(w):
        arrived(w_blocks(w, 0), w_in[w][0])
        for d, k in FROM:
            send(w_blocks(w, 0), w_blocks(w, k), z_hop[w][0][d], z_to[d])
        w_pass(w, 0)

    def z_second(w, d):
        k = FROM[d][1]
        arrived(w_blocks(w, k), z_hop[w][0][d])
        half = (128 * d, 128)
        send(w_blocks(w, k, *half), w_blocks(w, 2, *half), z_hop[w][1], z_to[d])
        w_pass(w, k)

    def z_last(w):
        arrived(w_blocks(w, 2), z_hop[w][1])
        w_pass(w, 2)

    def d_block(k, start=0, size=256):
        return wts.at[2, c, l, k, pl.ds(start, size), :]

    def d_first():
        for d, k in FROM:
            send(d_block(0), d_block(k), z_hop[2][0][d], z_to[d])
        send(d_block(0), d_block(0), w_in[2][0], l_to)

    def d_second(d):
        k = FROM[d][1]
        arrived(d_block(k), z_hop[2][0][d])
        half = (128 * d, 128)
        send(d_block(k, *half), d_block(2, *half), z_hop[2][1], z_to[d])
        send(d_block(k), d_block(k), w_in[2][k], l_to)

    def d_last():
        arrived(d_block(2), z_hop[2][1])
        send(d_block(2), d_block(2), w_in[2][2], l_to)

    def d_pass(k):
        arrived(wts.at[2, c, 1 - l, k], w_in[2][k])
        w_pass(2, k)

    def weight_ready(w, k):
        arrived(wts.at[w, 1 - c, :, k], pass_in[w][k])

    first_blocks = [(q, k) for q in range(2) for k in GATHER[:3]]
    last_blocks = [(q, GATHER[3]) for q in range(2)]

    def product(w, f, blocks):
        lhs = jnp.concatenate([xin[w // 2, q, k].reshape(512, 256) for q, k in blocks], axis=1)
        rhs = jnp.concatenate([wts[w, f, q, k] for q, k in blocks], axis=0)
        return dot(lhs, rhs, NN)

    def products(w):
        for f in range(2):
            part[w, f] = product(w, f, first_blocks)

    def activate(f):
        gate = part[0, f] + product(0, f, last_blocks)
        up = part[1, f] + product(1, f, last_blocks)
        back = part[2, f] + product(2, f, last_blocks)
        s = jax.nn.sigmoid(gate)
        silu = gate * s
        act[0, f] = (back * up * (s * (1.0 + gate * (1.0 - s)))).astype(BF16)
        act[1, f] = (back * silu).astype(BF16)
        act[2, f] = (silu * up).astype(BF16)

    ry1_in, rxb1_in = take(4), take(4)
    rxa1_in = [take(2) for _ in range(4)]
    last = [(0, k) for k in range(4)] + [(1, k) for k in CROSS_OUT]
    rxa0_in, rxb0_in, ry0_in = {q: take(2) for q in last}, {q: take() for q in last}, {q: take() for q in last}
    home_in = take(2)

    def backward(w, q, k):
        lhs = jnp.concatenate([act[w, 0], act[w, 1]], axis=1)
        return dot(lhs, jnp.concatenate([wts[w, 0, q, k], wts[w, 1, q, k]], axis=1), NT)

    def output(a, k):
        for q in range(2):
            r = backward(0, q, k) + backward(1, q, k) if a else backward(2, q, k)
            res[a, q, k] = r.astype(BF16).reshape(2, 256, 256)

    def group(a, k, g):
        return res.at[a, :, k, :, pl.ds(g * 64, 64), :]

    def half_group(a, k, g, r):
        return res.at[a, :, k, r, pl.ds(g * 64, 64), :]

    def slot(k, g, start=0, size=64):
        return res.at[1, :, k, 0, pl.ds(g * 64 + start, size), :]

    def step1(a, k):
        output(a, k)
        for d in range(2):
            send(half_group(a, k, 2, d), rxa0.at[a, d, :, k], rxa0_in[a, k][d], x_to[d])

    def step2(a, k, d):
        g = TO[d][1]
        arrived(rxa0.at[a, d, :, k], rxa0_in[a, k][d])
        add_into(half_group(a, k, g, d), rxa0.at[a, d, :, k])
        send(group(a, k, g), rxb0.at[a, d, :, k], rxb0_in[a, k], x_to[d])

    def step3(a, k):
        arrived(rxb0.at[a, :, :, k], rxb0_in[a, k])
        sy[a, :, k] = (
            res[a, :, k, 1, 0:64, :].astype(F32)
            + rxb0[a, 0, :, k, 1].astype(F32)
            + rxb0[a, 1, :, k, 1].astype(F32)
        ).astype(BF16)
        send(sy.at[a, :, k], ry0.at[a, :, k], ry0_in[a, k], y_to)

    home = [out_ref, gtok_ref]

    def go_home(a, k):
        dst = home[a].at[rows((p * 4 + z) * 64, 64), :]
        for dl in (1, 0):
            q = (l + dl) % 2
            if dl or k:
                send(fin.at[a, q, k], dst, home_in[a], dev(h, c, x, q, ring(z, k)))
            else:
                keep(fin.at[a, q, k], dst, home_in[a])

    def step4(a, k):
        arrived(ry0.at[a, :, k], ry0_in[a, k])
        fin[a, :, k] = (
            res[a, :, k, 0, 0:64, :].astype(F32)
            + rxb0[a, 0, :, k, 0].astype(F32)
            + rxb0[a, 1, :, k, 0].astype(F32)
            + ry0[a, :, k].astype(F32)
        ).astype(BF16)
        go_home(a, k)

    def slot0(k):
        output(1, k)
        send(res.at[1, :, k, 1], ry1.at[:, k], ry1_in[k], y_to)

    def slot1(k):
        arrived(ry1.at[:, k], ry1_in[k])
        add_into(res.at[1, :, k, 0], ry1.at[:, k])
        for d in range(2):
            send(slot(k, 2, 32 * d, 32), rxa1.at[d, :, k], rxa1_in[k][d], x_to[d])

    def slot2(k, d):
        g = TO[d][1]
        arrived(rxa1.at[d, :, k], rxa1_in[k][d])
        add_into(slot(k, g, 32 * d, 32), rxa1.at[d, :, k])
        send(slot(k, g), rxb1.at[d, :, k], rxb1_in[k], x_to[d])

    def slot3(k):
        arrived(rxb1.at[:, :, k], rxb1_in[k])
        fin[1, :, k] = (
            res[1, :, k, 0, 0:64, :].astype(F32)
            + rxb1[0, :, k].astype(F32)
            + rxb1[1, :, k].astype(F32)
        ).astype(BF16)
        go_home(1, k)

    sum_in = [take(4) for _ in range(3)]
    rza_in = [take(2) for _ in range(2)]
    rzb_in, gy_in = take(2), take(2)
    rza2_in, rzb2_in, gy2_in = take(2), take(), take(4)

    def grad0(w, k):
        for q in range(2):
            lhs = xin[w // 2, q, k].reshape(512, 256)
            wgo[w, q, k] = dot(lhs, act[w, 1 - c], TN).astype(BF16)
        send(wgo.at[w, :, k], wgi.at[w, :, k], sum_in[w][k], core_to)
        for q in range(2):
            lhs = xin[w // 2, q, k].reshape(512, 256)
            wgr[w, q, k] = dot(lhs, act[w, c], TN).astype(BF16)

    def both(w, k):
        arrived(wgi.at[w, :, k], sum_in[w][k])
        add_into(wgr.at[w, :, k], wgi.at[w, :, k])

    def grad1(w):
        both(w, 2)
        for d in range(2):
            send(wgr.at[w, :, 2, pl.ds(128 * d, 128), :], rza.at[w, d], rza_in[w][d], z_to[d])

    def grad2(w, d):
        k = TO[d][1]
        both(w, k)
        arrived(rza.at[w, d], rza_in[w][d])
        add_into(wgr.at[w, :, k, pl.ds(128 * d, 128), :], rza.at[w, d])
        send(wgr.at[w, :, k], rzb.at[w, d], rzb_in[w], z_to[d])

    def grad3(w):
        both(w, 0)
        arrived(rzb.at[w], rzb_in[w])
        gl[w] = (
            wgr[w, :, 0].astype(F32) + rzb[w, 0].astype(F32) + rzb[w, 1].astype(F32)
        ).astype(BF16)
        send(gl.at[w, 1 - l], gy.at[w], gy_in[w], l_to)

    def grad4(w):
        arrived(gy.at[w], gy_in[w])
        [ggate_ref, gup_ref][w][...] = gl[w, l].astype(F32) + gy[w].astype(F32)

    def down1(k):
        both(2, k)
        send(wgr.at[2, 1 - l, k], gy2.at[k], gy2_in[k], l_to)

    def down_sum(k):
        arrived(gy2.at[k], gy2_in[k])
        add_into(wgr.at[2, l, k], gy2.at[k])

    def down2():
        down_sum(2)
        for d in range(2):
            send(wgr.at[2, l, 2, pl.ds(128 * d, 128), :], rza2.at[d], rza2_in[d], z_to[d])

    def down3(d):
        k = TO[d][1]
        down_sum(k)
        arrived(rza2.at[d], rza2_in[d])
        add_into(wgr.at[2, l, k, pl.ds(128 * d, 128), :], rza2.at[d])
        send(wgr.at[2, l, k], rzb2.at[d], rzb2_in, z_to[d])

    def down4():
        down_sum(0)
        arrived(rzb2, rzb2_in)
        r = wgr[2, l, 0].astype(F32) + rzb2[0].astype(F32) + rzb2[1].astype(F32)
        gdown_ref[...] = r.T

    def finish():
        for a in (1, 0):
            arrived(home[a], home_in[a])

    for step, *args in (
        (scatter, 1, 0), (scatter, 1, 1), (scatter, 1, 3), (early, 0), (scatter, 1, 2), (scatter, 0, 0),
        (w_own, 0), (early, 1), (scatter, 0, 1), (scatter, 0, 3), (scatter, 0, 2), (w_own, 1), (d_first,),
        (x_in, 1, 0), (x_in, 1, 3), (x_in, 1, 1), (x_in, 1, 2), (x_in, 0, 0), (x_other, 1, 0),
        (x_second, 1, 0, 0, 0), (x_second, 1, 0, 0, 1), (x_second, 1, 0, 3, 0), (x_second, 1, 0, 3, 1),
        (z_first, 0), (x_second, 1, 0, 1, 0), (x_second, 1, 0, 1, 1), (x_in, 0, 3), (x_in, 0, 1),
        (x_second, 1, 0, 2, 0), (x_second, 1, 0, 2, 1), (d_second, 0), (d_second, 1), (x_second, 0, 0, 0, 0),
        (x_second, 0, 0, 0, 1), (weight_ready, 0, 0), (x_in, 0, 2), (x_other, 0, 0), (x_second, 1, 1, 0, 0),
        (x_second, 1, 1, 0, 1), (z_first, 1), (x_last, 3), (x_last, 1), (weight_ready, 1, 0),
        (x_second, 0, 0, 3, 0), (x_second, 0, 0, 3, 1), (d_pass, 0), (z_second, 0, 0), (z_second, 0, 1),
        (x_second, 0, 0, 1, 0), (x_second, 0, 0, 1, 1), (d_last,), (x_last, 2), (x_other, 0, 3),
        (weight_ready, 2, 0), (d_pass, 3), (weight_ready, 0, 3), (x_other, 0, 1), (weight_ready, 0, 1),
        (x_second, 0, 0, 2, 0), (x_second, 0, 0, 2, 1), (weight_ready, 2, 3), (x_second, 0, 1, 0, 0),
        (x_second, 0, 1, 0, 1), (d_pass, 1), (z_second, 1, 0), (z_second, 1, 1), (x_other, 0, 2),
        (weight_ready, 2, 1), (d_pass, 2), (x_second, 0, 1, 3, 0), (x_second, 0, 1, 3, 1),
        (weight_ready, 1, 3), (x_second, 0, 1, 1, 0), (x_second, 0, 1, 1, 1), (weight_ready, 1, 1),
        (z_last, 0), (weight_ready, 2, 2), (gathered, 0), (weight_ready, 0, 2), (x_second, 0, 1, 2, 0),
        (x_second, 0, 1, 2, 1), (z_last, 1), (gathered, 3), (gathered, 1), (products, 0), (products, 1),
        (weight_ready, 1, 2), (products, 2), (gathered, 2), (activate, 0), (activate, 1), (step1, 0, 2),
        (step1, 1, 2), (slot0, 1), (grad0, 0, 2), (slot0, 3), (step1, 0, 1), (step1, 0, 3), (grad0, 1, 2),
        (step2, 0, 2, 0), (grad1, 0), (step2, 0, 2, 1), (slot0, 0), (step2, 1, 2, 0), (step2, 1, 2, 1),
        (grad0, 2, 2), (step1, 0, 0), (grad1, 1), (grad0, 0, 1), (step2, 0, 1, 0), (step2, 0, 1, 1),
        (grad0, 0, 3), (grad0, 1, 1), (down1, 2), (step2, 0, 3, 0), (step2, 0, 3, 1), (grad0, 2, 1),
        (grad0, 1, 3), (grad0, 2, 3), (grad2, 0, 0), (grad2, 0, 1), (slot1, 1), (grad0, 0, 0), (grad0, 1, 0),
        (step3, 0, 2), (down1, 1), (grad0, 2, 0), (grad2, 1, 0), (down1, 3), (grad2, 1, 1), (down2,),
        (step3, 1, 2), (down1, 0), (slot1, 3), (step2, 0, 0, 0), (step2, 0, 0, 1), (step3, 0, 1), (grad3, 0),
        (slot1, 0), (step3, 0, 3), (slot2, 1, 0), (slot2, 1, 1), (step4, 0, 2), (slot2, 3, 0), (slot2, 3, 1),
        (step4, 1, 2), (grad3, 1), (down3, 0), (step4, 0, 1), (step3, 0, 0), (grad4, 0), (down3, 1),
        (slot2, 0, 0), (slot2, 0, 1), (step4, 0, 3), (slot3, 1), (slot3, 3), (step4, 0, 0), (grad4, 1),
        (slot3, 0), (down4,), (finish,),
    ):
        step(*args)
    for copy in pool:
        if copy is not None:
            copy.wait_send()


def place(*refs):
    held, sems = refs[10:15], refs[15]
    come = [pltpu.make_async_copy(refs[n], held[n], sems.at[n]) for n in range(5)]
    go = [pltpu.make_async_copy(held[n], refs[5 + n], sems.at[5 + n]) for n in range(5)]
    for copy in come:
        copy.start()
    for first, then in zip(come, go):
        first.wait()
        then.start()
    for copy in go:
        copy.wait()


def on_device(tokens, gate_weight, up_weight, down_weight, cotangent):
    vmem = pl.BlockSpec(memory_space=pltpu.VMEM)
    anywhere = pl.BlockSpec(memory_space=pl.ANY)
    shapes = [jax.ShapeDtypeStruct((512, 256), BF16)] * 2
    shapes += [jax.ShapeDtypeStruct((256, 256), F32)] * 3
    results = pl.pallas_call(
        kernel,
        name="swiglu",
        out_shape=shapes,
        in_specs=[anywhere] * 5,
        out_specs=[anywhere] * 2 + [vmem] * 3,
        scratch_shapes=[
            pltpu.VMEM((256, 256), BF16),
            pltpu.VMEM((2, 2, 4, 2, 256, 256), BF16),
            pltpu.VMEM((3, 2, 2, 4, 256, 256), BF16),
            pltpu.VMEM((3, 2, 512, 256), F32),
            pltpu.VMEM((3, 2, 512, 256), BF16),
            pltpu.VMEM((2, 2, 4, 2, 256, 256), BF16),
            pltpu.VMEM((3, 2, 4, 256, 256), BF16),
            pltpu.VMEM((3, 2, 4, 256, 256), BF16),
            pltpu.VMEM((3, 2, 4, 256, 256), BF16),
            pltpu.VMEM((2, 2, 2, 4, 64, 256), BF16),
            pltpu.VMEM((2, 2, 4, 32, 256), BF16),
            pltpu.VMEM((2, 2, 2, 4, 2, 64, 256), BF16),
            pltpu.VMEM((2, 2, 4, 64, 256), BF16),
            pltpu.VMEM((2, 2, 4, 64, 256), BF16),
            pltpu.VMEM((2, 4, 256, 256), BF16),
            pltpu.VMEM((2, 2, 4, 64, 256), BF16),
            pltpu.VMEM((2, 2, 4, 64, 256), BF16),
            pltpu.VMEM((2, 2, 2, 128, 256), BF16),
            pltpu.VMEM((2, 2, 2, 256, 256), BF16),
            pltpu.VMEM((2, 256, 256), BF16),
            pltpu.VMEM((2, 2, 256, 256), BF16),
            pltpu.VMEM((2, 128, 256), BF16),
            pltpu.VMEM((2, 256, 256), BF16),
            pltpu.VMEM((4, 256, 256), BF16),
            pltpu.SemaphoreType.DMA((N_SEND,)),
            pltpu.SemaphoreType.DMA((N_RECV,)),
            pltpu.SemaphoreType.DMA,
        ],
        compiler_params=pltpu.CompilerParams(
            collective_id=0, has_side_effects=True, vmem_limit_bytes=60 << 20
        ),
        cost_estimate=pl.CostEstimate(
            flops=9 * 2 * 1024 * 1024 * 512, bytes_accessed=3 << 20, transcendentals=1024 * 256
        ),
    )(
        tokens.reshape(512, 256),
        gate_weight,
        up_weight,
        down_weight,
        cotangent.reshape(512, 256),
    )
    output, grad_tokens, grad_gate, grad_up, grad_down = pl.pallas_call(
        place,
        name="place",
        out_shape=shapes,
        in_specs=[anywhere] * 5,
        out_specs=[anywhere] * 5,
        scratch_shapes=[pltpu.VMEM(s.shape, s.dtype) for s in shapes]
        + [pltpu.SemaphoreType.DMA((10,))],
    )(*results)
    return (
        output.reshape(2, 256, 256),
        grad_tokens.reshape(2, 256, 256),
        grad_gate,
        grad_up,
        grad_down,
    )


def solution(mesh):
    in_specs = (
        P(None, ("inp", "wt"), "out"),
        P("out", ("wt", "inp")),
        P("out", ("wt", "inp")),
        P(("wt", "inp"), "out"),
        P(None, ("inp", "wt"), "out"),
    )
    out_specs = (
        P(None, ("inp", "wt"), "out"),
        P(None, ("inp", "wt"), "out"),
        P("out", ("wt", "inp")),
        P("out", ("wt", "inp")),
        P(("wt", "inp"), "out"),
    )
    return jax.shard_map(
        on_device, mesh=mesh, in_specs=in_specs, out_specs=out_specs, check_vma=False
    )
```
